32 devices in a mesh: parts: 2 (over y), rows: 4 (over z), feat: 4 (over x, core).
Axes of the slice: x: 2, y: 2, z: 4, core: 2. Of those that a mesh axis runs over, the one named last changes fastest.
Arguments:
- tokens: bfloat16 [8192, 1024], P(('parts', 'rows')), parts along dimension 0
- cluster_id: int32 [8192, 1], P(('parts', 'rows')), parts along dimension 0, may hold values from 0 to 3; in each aligned block of 1024 rows (0 to 1023, 1024 to 2047, ...) at most 640 rows name the same one
- seeds: bfloat16 [8, 1024, 1024], P(('parts', 'rows'), 'feat'), parts along dimension 0
Outputs:
- centroids: bfloat16 [8, 1024, 1024], P(('parts', 'rows'), 'feat'), parts along dimension 0
- energy: float32 [8192], P(('parts', 'rows')), parts along dimension 0
The draws below stay inside these ranges and needn't reach their ends.
There are 2 independent parts, one for each index of `parts`. The reference program is written for one: setup_inputs(seed, part) draws one part's arguments, and reference() takes and returns one part's arrays. A program takes and returns all parts, laid end to end along the dimension named above; each array names one. Nothing has to cross between parts.
Inputs may be any that keep to these rules, and one draw needn't show every extreme that they name: `cluster_id`: each aligned block of 1024 rows (the rows of one index of rows) names one cluster at most 640 times.
All inputs are finite; a program needn't handle non-finite values.
Results may differ from the reference program's by a relative error of at most 0.0059.
Values may be sent and summed in bfloat16 or wider, within the bound.
A program may use at most 64 MiB of HBM per device.

```python
import math
import jax
import jax.numpy as jnp
import numpy as np
from jax import lax

D = 1024
K = 1024
ROW_DEV = 1024
ITERS = 2
NC = 4
CAP = 640
SLOTS = 2560
TOKENS = 4096
PROTOS = 128


def shared_directions(key):
    proto_key = jax.random.fold_in(key, 101)
    scale_key = jax.random.fold_in(key, 103)
    protos = jax.random.normal(proto_key, (PROTOS, D), jnp.float32)
    col_scale = jnp.exp(jax.random.uniform(scale_key, (1, D), jnp.float32) * math.log(4.0))
    return (protos, col_scale)


def draw_tokens(key, part):
    protos, col_scale = shared_directions(key)
    key = jax.random.fold_in(key, 7)
    keys = jax.random.split(key, 5)
    first = jax.random.randint(keys[3], (TOKENS,), 0, PROTOS)
    other = (first + jax.random.randint(keys[4], (TOKENS,), 1, PROTOS)) % PROTOS
    angle = jax.random.uniform(keys[1], (TOKENS, 1), jnp.float32, 0.18 * math.pi, 0.32 * math.pi)
    noise = 0.7 * jax.random.normal(keys[0], (TOKENS, D), jnp.float32)
    row_scale = jnp.exp(jax.random.uniform(keys[2], (TOKENS, 1), jnp.float32) * math.log(10.0))
    base = jnp.cos(angle) * protos[first] + jnp.sin(angle) * protos[other] + noise
    return (0.1 * base * row_scale * col_scale).astype(jnp.bfloat16)


def draw_seeds(key, part):
    protos, col_scale = shared_directions(key)
    key = jax.random.fold_in(key, 9)
    keys = jax.random.split(key, 3)
    ordered = jnp.arange(K, dtype=jnp.int32) * PROTOS // K
    shuffles = jax.vmap(lambda one: jax.random.permutation(one, K))(jax.random.split(keys[1], NC))
    which = ordered[shuffles]
    noise = 0.7 * jax.random.normal(keys[0], (NC, K, D), jnp.float32)
    row_scale = jnp.exp(jax.random.uniform(keys[2], (NC, K, 1), jnp.float32) * math.log(10.0))
    base = protos[which] + noise
    return (0.1 * base * row_scale * col_scale[None]).astype(jnp.bfloat16)


def routed_block(key, own, number, rows, count, top, bound, lean):
    sequence = jax.random.permutation(key, count)
    crowded, common = load_shares(count, rows * top, bound, lean, True), load_shares(count, rows * top, bound, lean, False)
    places = jnp.arange(count)

    def named(tallies, turn):
        used = int((tallies > 0).sum())
        fixed = max(1, used // 4)
        passed = fixed + (places - fixed + turn * (used - fixed)) % max(1, count - fixed)
        return jnp.zeros((count,), jnp.int32).at[sequence[jnp.where(places < fixed, places, passed)]].set(jnp.asarray(tallies, jnp.int32))

    tallies = jnp.where(number % 4 == 0, named(crowded, number // 4), named(common, number - number // 4 - 1))
    mixed = jax.random.permutation(jax.random.fold_in(own, 3), count)
    giver, taker = mixed[0:count // 2 * 2:2], mixed[1:count // 2 * 2:2]
    room = jnp.minimum(tallies[giver] - 1, bound - tallies[taker]) // 2
    room = jnp.where((giver == sequence[0]) | (taker == sequence[0]) | (tallies[taker] == 0), 0, jnp.maximum(room, 0))
    passed = jax.random.randint(jax.random.fold_in(own, 4), (count // 2,), 0, 1 << 20) % (room + 1)
    tallies = tallies.at[giver].add(-passed).at[taker].add(passed)
    items = jnp.searchsorted(jnp.cumsum(tallies), jnp.arange(rows * top), side="right").astype(jnp.int32)
    grid = items.reshape(top, rows).T
    grid = grid[jax.random.permutation(jax.random.fold_in(own, 1), rows)]
    turn = jax.random.randint(jax.random.fold_in(own, 2), (rows, 1), 0, top)
    return jnp.take_along_axis(grid, (jnp.arange(top)[None, :] + turn) % top, axis=1)


def load_shares(number_of, total, reach, slope, full):
    weights = [(1 << 20) // math.isqrt(standing ** slope) + 1 for standing in range(1, number_of + 1)]
    largest = reach if full else min(reach, max(-(-total // number_of), total * weights[0] // sum(weights)))
    least = 1 if total - largest >= number_of - 1 else 0
    given, surplus = [largest] + [least] * (number_of - 1), total - largest - least * (number_of - 1)
    while surplus > 0:
        movable = [i for i in range(1, number_of) if given[i] < largest] or [i for i in range(1, number_of) if given[i] < reach]
        mass, remaining = sum([weights[i] for i in movable]), surplus
        for i in movable:
            more = min(reach - given[i], max(1, remaining * weights[i] // mass), surplus)
            given[i] = given[i] + more
            surplus = surplus - more
    return np.array(given)


def setup_inputs(seed: int = 0, part: int = 0) -> dict:
    key_list = jax.random.split(jax.random.key(seed), 4)
    part_keys = jax.random.split(jax.random.fold_in(key_list[3], part), 4)
    tokens = draw_tokens(jax.random.fold_in(jax.random.fold_in(key_list[3], part), 71), part)
    cluster_id_keys = jax.random.split(jax.random.fold_in(part_keys[1], 1), TOKENS // ROW_DEV)
    cluster_id_turns = jax.random.permutation(jax.random.fold_in(part_keys[1], 3), TOKENS // ROW_DEV)
    cluster_id = jax.vmap(lambda own, number: routed_block(jax.random.fold_in(part_keys[1], 2), own, number, ROW_DEV, NC, 1, CAP, 2))(cluster_id_keys, cluster_id_turns).reshape((TOKENS, 1))
    seeds = draw_seeds(jax.random.fold_in(jax.random.fold_in(key_list[3], part), 71), part)
    return dict(tokens=tokens, cluster_id=cluster_id, seeds=seeds)


sharpness = 20.0
epsilon = 1e-06

def unit_rows(values):
    wide = values.astype(jnp.float32)
    return wide * lax.rsqrt(lax.optimization_barrier(jnp.sum(wide * wide, axis=-1, keepdims=True)) + epsilon)

def weights_of(members, current):
    cosine = jnp.dot(members, current.T, preferred_element_type=jnp.float32)
    weight = jnp.exp(sharpness * (cosine - 1.0))
    return (weight, lax.optimization_barrier(jnp.sum(weight, axis=1)))

def reference(tokens, cluster_id, seeds):
    unit = unit_rows(tokens).astype(jnp.bfloat16)
    labels = cluster_id[:, 0]
    order = jnp.argsort(labels, stable=True).astype(jnp.int32)
    counts = lax.optimization_barrier(jnp.sum((labels[:, None] == jnp.arange(NC, dtype=jnp.int32)[None, :]).astype(jnp.int32), axis=0))
    starts = (jnp.cumsum(counts) - counts).astype(jnp.int32)
    padded_order = jnp.concatenate([order, jnp.zeros((SLOTS,), jnp.int32)])

    def one_cluster(which):
        indices = lax.dynamic_slice_in_dim(padded_order, starts[which], SLOTS)
        valid = jnp.arange(SLOTS, dtype=jnp.int32) < counts[which]
        members = jnp.where(valid[:, None], unit[indices], jnp.zeros((), jnp.bfloat16))
        current = unit_rows(seeds[which]).astype(jnp.bfloat16)
        for step in range(ITERS):
            weight, total = weights_of(members, current)
            prob = (weight / total[:, None]).astype(jnp.bfloat16)
            moment = jnp.dot(prob.T, members, preferred_element_type=jnp.float32)
            current = unit_rows(moment).astype(jnp.bfloat16)
        weight, total = weights_of(members, current)
        energies = 1.0 + jnp.log(total) / sharpness
        return (current, energies, indices, valid)
    centroids, energies, indices, valid = lax.map(one_cluster, jnp.arange(NC, dtype=jnp.int32))
    picked = jnp.where(valid, energies, jnp.zeros((), jnp.float32)).reshape(-1)
    energy = jnp.zeros((TOKENS,), jnp.float32).at[indices.reshape(-1)].add(picked)
    return (centroids, energy)
```

```python
import functools

import jax
import jax.numpy as jnp
from jax import lax
from jax.experimental import pallas as pl
from jax.experimental.pallas import tpu as pltpu
from jax.sharding import PartitionSpec as P

ITERS = 2
LANES = 128
SUBLANES = 8
SHARPNESS = 20.0
EPSILON = 1e-06
MESH = pl.DeviceIdType.MESH
F32 = jnp.float32
BF16 = jnp.bfloat16


def unit_rows(wide):
    return wide * lax.rsqrt(jnp.sum(wide * wide, axis=-1, keepdims=True) + EPSILON)


def steps(low, high, body):
    if high - low <= 8:
        for k in range(low, high):
            body(k)
    else:
        pl.loop(low, high)(body)


def when(condition, body):
    if isinstance(condition, bool):
        if condition:
            body()
    else:
        pl.when(condition)(body)


def kernel(groups, feats, chunk, parts_of_chunk, tokens_ref, label_ref, seeds_ref, cent_ref, energy_ref,
           members, outgoing, current, weight, moment, totals, ending, endings,
           zsend, xsend, csend, fsend, arrive, tsend, trecv, esend, erecv):
    me = lax.axis_index("rows")
    ft = lax.axis_index("feat")
    far = lax.rem(ft + 2, feats)
    sib = ft + 1 - 2 * lax.rem(ft, 2)
    farsib = lax.rem(sib + 2, feats)
    own_rows = tokens_ref.shape[0]
    slots = feats * chunk
    sub = chunk // parts_of_chunk
    ranks8 = totals.shape[-2]
    nsplit = slots // LANES

    barrier = pltpu.get_barrier_semaphore()

    def greet(k):
        for j in range(feats):
            if isinstance(k, int) and k == 0 and j == 0:
                continue
            pl.semaphore_signal(
                barrier, inc=1,
                device_id={"rows": lax.rem(me + k, groups), "feat": lax.rem(ft + j, feats)},
                device_id_type=MESH)

    greet(0)
    steps(1, groups, greet)

    tri = (lax.broadcasted_iota(jnp.int32, (LANES, LANES), 0)
           < lax.broadcasted_iota(jnp.int32, (LANES, LANES), 1)).astype(BF16)
    high = max(SUBLANES, groups)
    carry = jnp.zeros((high, 1), F32)
    ranks = []
    for b in range(own_rows // LANES):
        lab = label_ref[:, b * LANES:(b + 1) * LANES]
        hit = lax.broadcasted_iota(jnp.int32, (high, LANES), 0) == lab
        hot = jnp.where(hit, 1.0, 0.0)
        before = jnp.dot(hot.astype(BF16), tri, preferred_element_type=F32) + carry
        ranks.append(jnp.sum(hot * before, axis=0, keepdims=True))
        carry = carry + jnp.sum(hot, axis=1, keepdims=True)
    rank = jnp.concatenate(ranks, axis=1).astype(jnp.int32)
    label = label_ref[...]
    slot = label * slots + rank

    def picked(base, count):
        hot = (lax.broadcasted_iota(jnp.int32, (count, own_rows), 0) + base == slot)
        rows = jnp.dot(jnp.where(hot, 1.0, 0.0).astype(BF16), tokens_ref[...], preferred_element_type=F32)
        return unit_rows(rows).astype(BF16)

    def span(quarter, h):
        return pl.ds(pl.multiple_of(quarter * chunk + h * sub, 16), sub)

    def zcopy(k, h, dest, source):
        return pltpu.make_async_remote_copy(
            src_ref=outgoing.at[k, pl.ds(h * sub, sub)], dst_ref=members.at[source, span(ft, h)],
            send_sem=zsend.at[k, h], recv_sem=arrive.at[source, ft, h],
            device_id={"rows": dest}, device_id_type=MESH)

    def fcopy(source, quarter, h, peer, sem):
        place = members.at[source, span(quarter, h)]
        return pltpu.make_async_remote_copy(
            src_ref=place, dst_ref=place, send_sem=sem.at[source, h], recv_sem=arrive.at[source, quarter, h],
            device_id={"feat": peer}, device_id_type=MESH)

    def send_out(k):
        dest = lax.rem(me + k, groups)
        outgoing[k] = picked(dest * slots + ft * chunk, chunk)
        if isinstance(k, int) and k == 1:
            pl.semaphore_wait(barrier, groups * feats - 1)
        for h in range(parts_of_chunk):
            zcopy(k, h, dest, me).start()

    send_out(1)
    steps(2, groups, send_out)
    members[me] = picked(me * slots, slots)
    current[...] = unit_rows(seeds_ref[...].astype(F32)).astype(BF16)

    def weigh(s):
        cosine = lax.dot_general(current[...], members[s], (((1,), (1,)), ((), ())), preferred_element_type=F32)
        return jnp.exp(SHARPNESS * (cosine - 1.0))

    def folded(w):
        t = jnp.sum(w, axis=0, keepdims=True)
        rows = [t[:, j * LANES:(j + 1) * LANES] for j in range(nsplit)]
        rows.append(jnp.ones((ranks8 - nsplit, LANES), F32))
        return jnp.concatenate(rows, axis=0)

    def tcopy(it, s, owner, j, peer):
        place = totals.at[it, owner, s]
        return pltpu.make_async_remote_copy(
            src_ref=place, dst_ref=place, send_sem=tsend.at[it, s, j], recv_sem=trecv.at[it, s, owner],
            device_id={"feat": peer}, device_id_type=MESH)

    peers = [lax.rem(ft + j, feats) for j in range(feats)]

    def cos_block(it, s):
        w = weigh(s)
        weight[s] = w
        totals[it, ft, s] = folded(w)
        for j in range(1, feats):
            tcopy(it, s, ft, j, peers[j]).start()

    def prob_block(it, s):
        for j in range(1, feats):
            tcopy(it, s, peers[j], j, peers[j]).wait_recv()
        total = totals[it, 0, s]
        for j in range(1, feats):
            total = total + totals[it, j, s]
        inverse = 1.0 / total
        cut = [(weight[s, :, j * LANES:(j + 1) * LANES] * inverse[j:j + 1, :]).astype(BF16) for j in range(nsplit)]
        return jnp.concatenate(cut, axis=1)

    def add_block(it, s):
        moment[...] += jnp.dot(prob_block(it, s), members[s], preferred_element_type=F32)

    moment[...] = jnp.zeros_like(moment)

    def source_of(k):
        return lax.rem(me - k + groups, groups)

    cos_block(0, me)

    def overlapped(k):
        def landed():
            s = source_of(k)
            for h in range(parts_of_chunk):
                zcopy(0, h, s, s).wait_recv()
                fcopy(s, ft, h, far, xsend).start()
                fcopy(s, ft, h, sib, csend).start()

        def crossed():
            s = source_of(k - 1)
            for h in range(parts_of_chunk):
                fcopy(s, far, h, far, xsend).wait_recv()
                fcopy(s, far, h, sib, fsend).start()

        def whole():
            s = source_of(k - 1)
            for h in range(parts_of_chunk):
                fcopy(s, sib, h, sib, csend).wait_recv()
                fcopy(s, farsib, h, sib, fsend).wait_recv()
            cos_block(0, s)

        when(k < groups, landed)
        when(k >= 2, crossed)
        when(k >= 2, whole)
        when(k >= 2, lambda: add_block(0, source_of(k - 2)))

    steps(1, groups + 1, overlapped)
    add_block(0, source_of(groups - 1))
    current[...] = unit_rows(moment[...]).astype(BF16)

    for it in range(1, ITERS):
        steps(0, groups, lambda k: cos_block(it, source_of(k)))
        moment[...] = jnp.zeros_like(moment)
        steps(0, groups, lambda k: add_block(it, source_of(k)))
        current[...] = unit_rows(moment[...]).astype(BF16)

    cent_ref[...] = current[...]

    def ecopy(k, j, sender_row, sender_feat, s, peer):
        return pltpu.make_async_remote_copy(
            src_ref=ending.at[s], dst_ref=endings.at[sender_feat, sender_row],
            send_sem=esend.at[k, j], recv_sem=erecv.at[sender_feat, sender_row],
            device_id={"rows": s, "feat": peer}, device_id_type=MESH)

    def end_block(k):
        s = source_of(k)
        value = folded(weigh(s))
        ending[s] = value
        first = 0
        if isinstance(k, int) and k == 0:
            endings[ft, me] = value
            first = 1
        for j in range(first, feats):
            ecopy(k, j, me, ft, s, peers[j]).start()

    steps(1, groups, end_block)
    end_block(0)

    def end_wait(k):
        s = source_of(k)
        for j in range(1 if isinstance(k, int) and k == 0 else 0, feats):
            ecopy(k, j, s, peers[j], s, peers[j]).wait_recv()

    steps(1, groups, end_wait)
    end_wait(0)
    total = endings[0]
    for j in range(1, feats):
        total = total + endings[j]
    energy = (1.0 + jnp.log(total) / SHARPNESS).reshape(groups * ranks8, LANES)
    lead = energy.astype(BF16)
    rest = energy - lead.astype(F32)
    mid = rest.astype(BF16)
    low = (rest - mid.astype(F32)).astype(BF16)
    lane = jnp.where(lax.broadcasted_iota(jnp.int32, (LANES, own_rows), 0) == lax.rem(rank, LANES), 1.0, 0.0).astype(BF16)
    taken = (jnp.dot(lead, lane, preferred_element_type=F32)
             + jnp.dot(mid, lane, preferred_element_type=F32)
             + jnp.dot(low, lane, preferred_element_type=F32))
    line = lax.broadcasted_iota(jnp.int32, (groups * ranks8, own_rows), 0) == label * ranks8 + lax.div(rank, LANES)
    energy_ref[...] = jnp.sum(jnp.where(line, taken, 0.0), axis=0, keepdims=True)

    def drain(k):
        s = source_of(k)
        for h in range(parts_of_chunk):
            zcopy(k, h, s, me).wait_send()
            fcopy(s, ft, h, far, xsend).wait_send()
            fcopy(s, ft, h, sib, csend).wait_send()
            fcopy(s, far, h, sib, fsend).wait_send()

    def drain_small(k):
        s = source_of(k)
        for it in range(ITERS):
            for j in range(1, feats):
                tcopy(it, s, ft, j, peers[j]).wait_send()
        for j in range(1 if isinstance(k, int) and k == 0 else 0, feats):
            ecopy(k, j, me, ft, s, peers[j]).wait_send()

    steps(1, groups, drain)
    steps(1, groups, drain_small)
    drain_small(0)


def on_device(tokens, cluster_id, seeds):
    own_rows, depth = tokens.shape
    groups = lax.axis_size("rows")
    feats = lax.axis_size("feat")
    fine = seeds.shape[1]
    capacity = (5 * own_rows + 2 * groups - 1) // (2 * groups)
    chunk = -(-capacity // (feats * 32)) * 32
    pieces = 2
    slots = feats * chunk
    ranks8 = -(-(slots // LANES + 1) // SUBLANES) * SUBLANES
    sem = pltpu.SemaphoreType.DMA
    vmem = pl.BlockSpec(memory_space=pltpu.VMEM)
    centroids, energy = pl.pallas_call(
        functools.partial(kernel, groups, feats, chunk, pieces),
        out_shape=(jax.ShapeDtypeStruct((fine, depth), BF16), jax.ShapeDtypeStruct((1, own_rows), F32)),
        in_specs=[vmem, vmem, vmem],
        out_specs=(vmem, vmem),
        scratch_shapes=[
            pltpu.VMEM((groups, slots, depth), BF16),
            pltpu.VMEM((groups, chunk, depth), BF16),
            pltpu.VMEM((fine, depth), BF16),
            pltpu.VMEM((groups, fine, slots), F32),
            pltpu.VMEM((fine, depth), F32),
            pltpu.VMEM((ITERS, feats, groups, ranks8, LANES), F32),
            pltpu.VMEM((groups, ranks8, LANES), F32),
            pltpu.VMEM((feats, groups, ranks8, LANES), F32),
            sem((groups, pieces)), sem((groups, pieces)), sem((groups, pieces)), sem((groups, pieces)),
            sem((groups, feats, pieces)),
            sem((ITERS, groups, feats)), sem((ITERS, groups, feats)),
            sem((groups, feats)), sem((feats, groups)),
        ],
        compiler_params=pltpu.CompilerParams(
            collective_id=0, has_side_effects=True, vmem_limit_bytes=56 * 1024 * 1024),
    )(tokens, cluster_id.reshape(1, own_rows), seeds[0])
    return centroids[None], energy.reshape(own_rows)


def solution(mesh):
    in_specs = (
        P(("parts", "rows"), None),
        P(("parts", "rows"), None),
        P(("parts", "rows"), "feat", None),
    )
    out_specs = (P(("parts", "rows"), "feat", None), P(("parts", "rows")))
    return jax.shard_map(
        on_device, mesh=mesh, in_specs=in_specs, out_specs=out_specs, check_vma=False
    )
```
